256 devices in a mesh: row: 16 (over z_lo, y), col: 4 (over x), depth: 4 (over z_hi, core).
Axes of the slice: x: 4, y: 4, z: 8 (z_hi: 2, z_lo: 4; z = z_hi * 4 + z_lo), core: 2. Of those that a mesh axis runs over, the one named last changes fastest.
Arguments:
- left_blocks: float32 [16384, 16, 2048], P('row', ('col', 'depth')), may hold values from -0.125 to 0.125
- left_pattern: int32 [128, 16, 16], P('row', ('col', 'depth')), may hold values 0 or 1
- right_window: float32 [16, 2048, 2048], P(('col', 'depth'), 'row'), may hold values from -6 to 6
- right_pattern: int32 [16, 16, 16], P(('col', 'depth'), 'row'), may hold values 0 or 1
- subset_cols: int32 [8], replicated, may hold values from 0 to 15, as said below
- square_cols: float32 [16384, 1024], P(('row', 'col', 'depth')), may hold values from -4 to 4
Outputs:
- purified: float32 [16384, 1024], P(('row', 'col', 'depth'))
The draws below stay inside these ranges and needn't reach their ends.
Inputs may be any that keep to these rules, and one draw needn't show every extreme that they name: `subset_cols`: 8 different block-column numbers of the window.
All inputs are finite; a program needn't handle non-finite values. No bound on the sum of `left_pattern` or of `right_pattern` on one device may be relied on, other than what follows from the above.
Results may differ from the reference program's by a relative error of at most 0.0001.
Values sent between devices are 32-bit elements; how exact they have to be, the bound alone decides.
A program may use at most 128 MiB of HBM per device.

```python
import jax
import jax.numpy as jnp
from jax import lax

BS = 128
NB = 256
WB = 16
SUB = 8
KG = 16
KR = 16
BR = 128


def draw_subset_cols(key, part):
    key = jax.random.fold_in(key, 7)
    order = jax.random.permutation(key, WB)
    return order[:SUB].astype(jnp.int32)


def with_ends(array, stream_key, smallest, largest):
    longest = array.shape.index(max(array.shape))
    spots = []
    for shift in (0, 1):
        where = [jax.random.randint(jax.random.fold_in(stream_key, axis), (), 0, length) for axis, length in enumerate(array.shape)]
        where[longest] = (where[longest] + shift) % array.shape[longest]
        spots.append(tuple(where))
    return array.at[spots[0]].set(smallest).at[spots[1]].set(largest)


def level_of(rng, extent, cuts, least, top_value):
    def one(position, parts):
        draws = jax.random.uniform(jax.random.fold_in(jax.random.fold_in(rng, 6), position), (parts,), jnp.float32, least / len(cuts), top_value / len(cuts))
        return jnp.repeat(jnp.exp(draws), extent[position] // parts).reshape((-1,) + (1,) * (len(extent) - position - 1))

    factor_of = one(*cuts[0])
    for cut in cuts[1:]:
        factor_of = factor_of * one(*cut)
    return factor_of


def gaussian(stream_key, shape, scale, reach, split=(), kind=jnp.bfloat16):
    level = level_of(stream_key, shape, split, -0.22, 0.18) if split else 1.0
    drawn = jax.random.normal(stream_key, shape, jnp.float32) * scale * level
    return jnp.minimum(jnp.maximum(drawn, -reach), reach).astype(kind)


def setup_inputs(seed: int = 0) -> dict:
    splits = jax.random.split(jax.random.key(seed), 7)
    return {
        "left_blocks": gaussian(splits[0], (BR * BS, KG, KR * BS), (NB * BS // 16) ** -0.5, 0.125, ((0, 16), (1, 16)), jnp.float32),
        "left_pattern": with_ends((jax.random.randint(splits[1], (BR, KG, KR), 0, 4) < 1).astype(jnp.int32), jax.random.fold_in(splits[1], 1), 0, 1),
        "right_window": gaussian(splits[2], (KG, KR * BS, WB * BS), 1.0, 6.0, ((0, 16), (1, 16)), jnp.float32),
        "right_pattern": with_ends((jax.random.randint(splits[3], (KG, KR, WB), 0, 4) < 1).astype(jnp.int32), jax.random.fold_in(splits[3], 1), 0, 1),
        "subset_cols": draw_subset_cols(jax.random.fold_in(splits[6], 71), 0),
        "square_cols": gaussian(splits[5], (BR * BS, SUB * BS), 0.5, 4.0, ((0, 256),), jnp.float32),
    }


def expand(pattern, block, dtype):
    grown = jnp.repeat(pattern.astype(dtype), block, axis=0)
    return jnp.repeat(grown, block, axis=1)


def reference(left_blocks, left_pattern, right_window, right_pattern, subset_cols, square_cols):
    height = left_blocks.shape[0]
    width = SUB * BS

    def step(total, slice_index):
        blocks = left_blocks[:, slice_index, :]
        pattern = left_pattern[:, slice_index, :]
        window = right_window[slice_index]
        wpattern = right_pattern[slice_index]
        masked = blocks * expand(pattern, BS, blocks.dtype)
        right = window * expand(wpattern, BS, window.dtype)
        shaped = right.reshape(right.shape[0], WB, BS)
        chosen = jnp.take(shaped, subset_cols, axis=1).reshape(right.shape[0], width)
        product = jnp.dot(masked, chosen, precision=lax.Precision.HIGHEST, preferred_element_type=jnp.float32)
        return total + product, None

    start = jnp.zeros((height, width), jnp.float32)
    cube, _ = lax.scan(step, start, jnp.arange(KG, dtype=jnp.int32))
    return 3.0 * square_cols - 2.0 * cube
```

```python
import functools

import jax
import jax.numpy as jnp
from jax import lax
from jax.experimental import pallas as pl
from jax.experimental.pallas import tpu as pltpu
from jax.sharding import PartitionSpec as P

MESH = pl.DeviceIdType.MESH
BS = 128
NH = 4
NW = 8
NR = 16


def dot_nt(a, b):
    return lax.dot_general(a, b, (((1,), (1,)), ((), ())), preferred_element_type=jnp.float32)


def kernel(cz, cy, left_h, lp_s, win_h, rp_s, sub_s, sq_v, out_v, flag_v, *scratch):
    (left_v, win_v, ahi, alo, spread, pt_v, idx_v, idx_s, bhi, blo,
     cs, cr, ps, xr, vz, zx, fl_a, fl_b, fl_c, fl_x, fl_z,
     rec0, rec1, rec2, rec3, zr0, zr1, zr2, zr3, yr0, yr1, yr2, yr3,
     wsem, lsem, pt_ss, pt_rs, a_ss, a_rs, z_ss, z_rs, y_ss, y_rs, f_ss, f_rs,
     c_ss, c_rs, x_ss, x_rs, v_ss, v_rs, fl_ss, fl_rs) = scratch
    rec = (rec0, rec1, rec2, rec3)
    zr = (zr0, zr1, zr2, zr3)
    yr = (yr0, yr1, yr2, yr3)
    half = cy // 2

    r = lax.axis_index("row")
    x = lax.axis_index("col")
    d = lax.axis_index("depth")
    y = lax.rem(r, 4)
    z = r // 4
    core = lax.rem(d, 2)
    zh = d // 2

    def row_at(dz, dy):
        return lax.rem(z + dz, 4) * 4 + lax.rem(y + dy, 4)

    core_peer = {"depth": d + 1 - 2 * core}
    zh_peer = {"depth": lax.rem(d + 2, 4)}

    def x_peer(dx):
        return {"col": lax.rem(x + dx, 4)}

    def remote(src, dst, ss, rs, device):
        return pltpu.make_async_remote_copy(
            src_ref=src, dst_ref=dst, send_sem=ss, recv_sem=rs, device_id=device, device_id_type=MESH
        )

    win_copies = []
    for w in range(16):
        cp = pltpu.make_async_copy(win_h.at[:, pl.ds(w * BS, BS)], win_v.at[w], wsem.at[w])
        cp.start()
        win_copies.append(cp)
    left_copies = []
    for part in range(4):
        cp = pltpu.make_async_copy(
            left_h.at[pl.ds(part * 4096, 4096)], left_v.at[pl.ds(part * 4096, 4096)], lsem.at[1 + part]
        )
        cp.start()
        left_copies.append(cp)
    barrier = pltpu.get_barrier_semaphore()
    for k in range(1, NR):
        pl.semaphore_signal(barrier, inc=1, device_id={"row": lax.rem(r + k, NR)}, device_id_type=MESH)
    for k in range(1, 4):
        pl.semaphore_signal(barrier, inc=1, device_id=x_peer(k), device_id_type=MESH)
    pl.semaphore_signal(barrier, inc=1, device_id=core_peer, device_id_type=MESH)
    pl.semaphore_signal(barrier, inc=1, device_id=zh_peer, device_id_type=MESH)

    lane = lax.broadcasted_iota(jnp.int32, (8, 128), 1)
    mine = jnp.zeros((8, 128), jnp.int32)
    for w in range(NW):
        mine = jnp.where(lane == r * NW + w, rp_s[0, sub_s[w]], mine)
    pt_v[r] = mine
    pl.semaphore_wait(barrier, 20)

    pt = []
    for k in range(1, NR):
        to = lax.rem(r + k, NR)
        cp = remote(pt_v.at[r], pt_v.at[r], pt_ss.at[k], pt_rs.at[k], {"row": to})
        cp.start()
        pt.append(cp)

    for cp in win_copies:
        cp.wait()
    for w in range(NW):
        block = win_v[sub_s[w]].T
        for h in range(NH):
            for to in range(4):
                at = 32 * h + 8 * to
                spread[h, to, w] = block[at:at + 8, :]
    a2a = []
    for h in range(NH):
        row = []
        for dy in (1, 3, 2):
            to = lax.rem(y + dy, 4)
            cp = remote(spread.at[h, to], rec[h].at[pl.ds(y * NW, NW)], a_ss.at[h, dy], a_rs.at[h, dy], {"row": row_at(0, dy)})
            cp.start()
            row.append(cp)
        a2a.append(row)
        rec[h][pl.ds(y * NW, NW)] = spread[h, y]

    def prepare(part):
        left_copies[part].wait()

        def body(i, _):
            piece = part * 4 + i
            at = lax.rem(piece, 2) * 512 + (piece // 4) * 128 + lax.rem(piece // 2, 2) * 64
            at = pl.multiple_of(at, 64)
            for q in range(NR):
                v = left_v[pl.ds(piece * 1024 + q, 64, stride=16), :]
                v = jnp.where(jnp.full((64, 128), lp_s[piece // 2, q], jnp.int32) != 0, v, 0.0)
                hi = v.astype(jnp.bfloat16)
                ahi[pl.ds(at, 64), q * BS:(q + 1) * BS] = hi
                alo[pl.ds(at, 64), q * BS:(q + 1) * BS] = (v - hi.astype(jnp.float32)).astype(jnp.bfloat16)
            return 0

        lax.fori_loop(0, 4, body, 0)

    prepare(0)

    for cp in pt:
        cp.wait_recv()
    pat = pt_v[0]
    for k in range(1, NR):
        pat = pat + pt_v[k]
    in_pool = lax.rem(lane, 32)
    c32 = pat
    for s in (1, 2, 4, 8, 16):
        c32 = c32 + jnp.where(in_pool >= s, pltpu.roll(c32, s, 1), 0)
    call = pat
    for s in (1, 2, 4, 8, 16, 32, 64):
        call = call + jnp.where(lane >= s, pltpu.roll(call, s, 1), 0)
    rank32 = c32 - pat
    rank = call - pat
    zsrc = (lane // 32) * cz + jnp.minimum(rank32, cz - 1)

    def column(v):
        return jnp.broadcast_to(v[0:1, :], (128, 128)).T

    blk = lax.broadcasted_iota(jnp.int32, (128, 128), 0)
    slot = lax.broadcasted_iota(jnp.int32, (128, 128), 1)
    on = column(pat) != 0
    first = jnp.where(on & (column(rank32) == slot) & (blk // 32 == z), blk - 32 * z, 0)
    second = jnp.where(on & (column(rank) == slot), column(zsrc), 0)
    idx_v[0:1, :] = jnp.sum(first, axis=0, keepdims=True)
    idx_v[1:2, :] = jnp.sum(second, axis=0, keepdims=True)
    idx_v[2:3, :] = jnp.minimum(rank, cy - 1)[0:1, :]
    idx_v[3:4, :] = pat[0:1, :]
    idx_v[4:8, :] = pat[0:4, :]
    over = jnp.where((in_pool == 31) & (c32 > cz), 1, 0) + jnp.where((lane == 127) & (call > cy), 1, 0)
    for s in (1, 2, 4, 8, 16, 32, 64):
        over = over + pltpu.roll(over, s, 1)
    fl_a[...] = over
    to_s = pltpu.make_async_copy(idx_v, idx_s, lsem.at[5])
    to_s.start()
    to_s.wait()

    zg = []
    for h in range(NH):
        for cp in a2a[h]:
            cp.wait_recv()

        def pack(j, _, h=h):
            at = idx_s[0, j]
            zr[h][z * cz + j] = rec[h][at]
            return 0

        if cz <= 20:
            for j in range(cz):
                pack(j, 0)
        else:
            lax.fori_loop(0, cz, pack, 0)
        row = []
        for dz in (1, 3, 2):
            part = zr[h].at[pl.ds(z * cz, cz)]
            cp = remote(part, part, z_ss.at[h, dz], z_rs.at[h, dz], {"row": row_at(dz, 0)})
            cp.start()
            row.append(cp)
        zg.append(row)

    yg, fg = {}, {}

    def y_send(h):
        for cp in zg[h]:
            cp.wait_recv()

        def pack(j, _):
            at = idx_s[1, j]
            yr[h][y, j] = zr[h][at]
            return 0

        if cy <= 64:
            def five(i, _):
                for k in range(10):
                    pack(i * 10 + k, 0)
                return 0

            lax.fori_loop(0, cy // 10, five, 0)
        else:
            lax.fori_loop(0, cy, pack, 0)
        for side, dy in ((0, 1), (1, 3)):
            for k in ((0, 1) if side == 0 else (1, 0)):
                part = yr[h].at[y, pl.ds(k * half, half)]
                cp = remote(part, part, y_ss.at[h, side, k], y_rs.at[h, side, k], {"row": row_at(0, dy)})
                cp.start()
                yg[h, side, k] = cp

    def y_forward(h):
        for side, dy in ((0, 1), (1, 3)):
            yg[h, side, side].wait_recv()
            part = yr[h].at[lax.rem(y + (3 if side == 0 else 1), 4), pl.ds(side * half, half)]
            cp = remote(part, part, f_ss.at[h, side], f_rs.at[h, side], {"row": row_at(0, dy)})
            cp.start()
            fg[h, side] = cp

    def expand(h):
        for side in (0, 1):
            yg[h, side, 1 - side].wait_recv()
            fg[h, side].wait_recv()

        def body(w, _):
            at = pl.multiple_of(w * 32, 32)
            for q in range(NR):
                place = idx_s[2, q * NW + w]
                keep = jnp.full((32, 128), idx_s[3, q * NW + w], jnp.int32) != 0
                v = jnp.concatenate([yr[h][k, place] for k in range(4)], axis=0)
                v = jnp.where(keep, v, 0.0)
                hi = v.astype(jnp.bfloat16)
                bhi[pl.ds(at, 32), q * BS:(q + 1) * BS] = hi
                blo[pl.ds(at, 32), q * BS:(q + 1) * BS] = (v - hi.astype(jnp.float32)).astype(jnp.bfloat16)
            return 0

        lax.fori_loop(0, NW, body, 0)

    def product(which):
        at = pl.multiple_of(which * 512, 512)
        a_hi, a_lo = ahi[pl.ds(at, 512), :], alo[pl.ds(at, 512), :]
        b_hi, b_lo = bhi[...], blo[...]
        return dot_nt(a_hi, b_hi) + dot_nt(a_hi, b_lo) + dot_nt(a_lo, b_hi)

    cg, xg, vg, flg = {}, {}, {}, {}

    def other_half(h):
        cs[h] = product(1 - core)
        cg[h] = remote(cs.at[h], cr.at[h], c_ss.at[h], c_rs.at[h], core_peer)
        cg[h].start()
        if h == 0:
            flg[0] = remote(fl_a, fl_c, fl_ss.at[0], fl_rs.at[0], core_peer)
            flg[0].start()

    def own_half(h):
        ps[h] = product(core)

    def over_x(h):
        cg[h].wait_recv()
        ps[h] = ps[h] + cr[h]
        for dx in (1, 3, 2):
            to = lax.rem(x + dx, 4)
            part = ps.at[h, pl.ds(pl.multiple_of(to * 128, 128), 128)]
            xg[h, dx] = remote(part, xr.at[h, dx - 1], x_ss.at[h, dx], x_rs.at[h, dx], x_peer(dx))
            xg[h, dx].start()
        if h == 0:
            flg[0].wait_recv()
            fl_b[0] = fl_a[...] + fl_c[...]
            for dx in (1, 3, 2):
                flg[dx] = remote(fl_b.at[0], fl_x.at[dx - 1], fl_ss.at[dx], fl_rs.at[dx], x_peer(dx))
                flg[dx].start()

    def over_zh(h):
        for dx in (1, 3, 2):
            xg[h, dx].wait_recv()
        own = ps[h, pl.ds(pl.multiple_of(x * 128, 128), 128), :]
        vz[h] = (own + xr[h, 0]) + (xr[h, 1] + xr[h, 2])
        part = vz.at[h, pl.ds(pl.multiple_of((1 - zh) * 64, 64), 64)]
        vg[h] = remote(part, zx.at[h], v_ss.at[h], v_rs.at[h], zh_peer)
        vg[h].start()
        if h == 0:
            for dx in (1, 3, 2):
                flg[dx].wait_recv()
            fl_b[1] = (fl_b[0] + fl_x[0]) + (fl_x[1] + fl_x[2])
            flg[4] = remote(fl_b.at[1], fl_z, fl_ss.at[4], fl_rs.at[4], zh_peer)
            flg[4].start()

    lane64 = lax.broadcasted_iota(jnp.int32, (64, 128), 1)

    def finish(h):
        vg[h].wait_recv()
        total = vz[h, pl.ds(pl.multiple_of(zh * 64, 64), 64), :] + zx[h]
        for w in range(NW):
            tile = total[:, (w // 4) * 128:(w // 4 + 1) * 128]
            shift = (32 * h - 32 * (w % 4)) % 128
            if shift:
                tile = pltpu.roll(tile, shift, 1)
            cols = slice(w * BS, (w + 1) * BS)
            value = 3.0 * sq_v[:, cols] - 2.0 * tile
            if h:
                value = jnp.where(lane64 // 32 == h, value, out_v[:, cols])
            out_v[:, cols] = value
        if h == 0:
            flg[4].wait_recv()
            flag_v[...] = fl_b[1] + fl_z[...]

    for part in range(1, 4):
        prepare(part)
    y_send(0)
    y_forward(0)
    for h in range(NH):
        if h + 1 < NH:
            y_send(h + 1)
        expand(h)
        other_half(h)
        if h + 1 < NH:
            y_forward(h + 1)
        own_half(h)
        over_x(h)
        if h >= 1:
            over_zh(h - 1)
        if h >= 2:
            finish(h - 2)
    finish(NH - 2)
    over_zh(NH - 1)
    finish(NH - 1)

    for cp in pt:
        cp.wait_send()
    for row in a2a + zg:
        for cp in row:
            cp.wait_send()
    for group in (yg, fg, cg, xg, vg, flg):
        for cp in group.values():
            cp.wait_send()


def run(cz, cy, collective_id, left, lp, win, rp, sub, sq):
    any_ = pl.BlockSpec(memory_space=pl.ANY)
    vmem = pl.BlockSpec(memory_space=pltpu.VMEM)
    smem = pl.BlockSpec(memory_space=pltpu.SMEM)
    f32, bf16, i32 = jnp.float32, jnp.bfloat16, jnp.int32
    dma = pltpu.SemaphoreType.DMA
    scratch = [
        pltpu.VMEM((16384, 128), f32),
        pltpu.VMEM((16, 128, 128), f32),
        pltpu.VMEM((1024, 2048), bf16),
        pltpu.VMEM((1024, 2048), bf16),
        pltpu.VMEM((NH, 4, NW, 8, 128), f32),
        pltpu.VMEM((NR, 8, 128), i32),
        pltpu.VMEM((8, 128), i32),
        pltpu.SMEM((8, 128), i32),
        pltpu.VMEM((256, 2048), bf16),
        pltpu.VMEM((256, 2048), bf16),
        pltpu.VMEM((NH, 512, 256), f32),
        pltpu.VMEM((NH, 512, 256), f32),
        pltpu.VMEM((NH, 512, 256), f32),
        pltpu.VMEM((NH, 3, 128, 256), f32),
        pltpu.VMEM((NH, 128, 256), f32),
        pltpu.VMEM((NH, 64, 256), f32),
        pltpu.VMEM((8, 128), i32),
        pltpu.VMEM((2, 8, 128), i32),
        pltpu.VMEM((8, 128), i32),
        pltpu.VMEM((3, 8, 128), i32),
        pltpu.VMEM((8, 128), i32),
    ]
    scratch += [pltpu.VMEM((4 * NW, 8, 128), f32) for _ in range(NH)]
    scratch += [pltpu.VMEM((4 * cz, 8, 128), f32) for _ in range(NH)]
    scratch += [pltpu.VMEM((4, cy, 8, 128), f32) for _ in range(NH)]
    scratch += [
        dma((16,)), dma((6,)),
        dma((NR,)), dma((NR,)),
        dma((NH, 4)), dma((NH, 4)),
        dma((NH, 4)), dma((NH, 4)),
        dma((NH, 2, 2)), dma((NH, 2, 2)),
        dma((NH, 2)), dma((NH, 2)),
        dma((NH,)), dma((NH,)),
        dma((NH, 4)), dma((NH, 4)),
        dma((NH,)), dma((NH,)),
        dma((5,)), dma((5,)),
    ]
    return pl.pallas_call(
        functools.partial(kernel, cz, cy),
        out_shape=(jax.ShapeDtypeStruct((64, 1024), f32), jax.ShapeDtypeStruct((8, 128), i32)),
        in_specs=[any_, smem, any_, smem, smem, vmem],
        out_specs=(vmem, vmem),
        scratch_shapes=scratch,
        compiler_params=pltpu.CompilerParams(
            collective_id=collective_id, has_side_effects=True, vmem_limit_bytes=56 * 2**20
        ),
    )(left, lp, win, rp, sub, sq)


def shards(left_blocks, left_pattern, right_window, right_pattern, subset_cols, square_cols):
    args = (
        left_blocks.reshape(1024 * NR, BS),
        left_pattern.reshape(8, NR),
        right_window.reshape(128, 2048),
        right_pattern.reshape(1, 16),
        subset_cols,
        square_cols,
    )
    fast, flag = run(18, 50, 0, *args)
    return lax.cond(
        flag[0, 0] > 0,
        lambda value, *rest: run(32, 128, 1, *rest)[0],
        lambda value, *rest: value,
        fast, *args,
    )


def solution(mesh):
    return jax.shard_map(
        shards,
        mesh=mesh,
        in_specs=(
            P("row", ("col", "depth"), None),
            P("row", ("col", "depth"), None),
            P(("col", "depth"), "row", None),
            P(("col", "depth"), "row", None),
            P(),
            P(("row", "col", "depth"), None),
        ),
        out_specs=P(("row", "col", "depth"), None),
        check_vma=False,
    )
```

```python
import functools

import jax
import jax.numpy as jnp
from jax import lax
from jax.experimental import pallas as pl
from jax.experimental.pallas import tpu as pltpu
from jax.sharding import PartitionSpec as P

MESH = pl.DeviceIdType.MESH
BS = 128
NH = 4
NW = 8
NR = 16


def dot_nt(a, b):
    return lax.dot_general(a, b, (((1,), (1,)), ((), ())), preferred_element_type=jnp.float32)


def kernel(cz, cy, left_h, lp_h, win_h, rp_h, sub_h, sq_h, out_v, flag_s, *scratch):
    (lp_s, rp_s, sub_s, sq_v, left_v, win_v, ahi, alo, spread, py_v, pz_v, one_v, one_s, idx_v, idx_s, bhi, blo,
     prod, cr, xr, vz, zx, fl_a, fl_b, fl_c, fl_x, fl_z,
     rec0, rec1, rec2, rec3, zr0, zr1, zr2, zr3, yr0, yr1, yr2, yr3,
     ssem, wsem, lsem, py_ss, py_rs, pz_ss, pz_rs, a_ss, a_rs, z_ss, z_rs, y_ss, y_rs, f_ss, f_rs,
     c_ss, c_rs, x_ss, x_rs, v_ss, v_rs, fl_ss, fl_rs) = scratch
    rec = (rec0, rec1, rec2, rec3)
    zr = (zr0, zr1, zr2, zr3)
    yr = (yr0, yr1, yr2, yr3)
    half = cy // 2

    r = lax.axis_index("row")
    x = lax.axis_index("col")
    d = lax.axis_index("depth")
    y = lax.rem(r, 4)
    z = r // 4
    core = lax.rem(d, 2)
    zh = d // 2

    def row_at(dz, dy):
        return lax.rem(z + dz, 4) * 4 + lax.rem(y + dy, 4)

    core_peer = {"depth": d + 1 - 2 * core}
    zh_peer = {"depth": lax.rem(d + 2, 4)}

    def x_peer(dx):
        return {"col": lax.rem(x + dx, 4)}

    def remote(src, dst, ss, rs, device):
        return pltpu.make_async_remote_copy(
            src_ref=src, dst_ref=dst, send_sem=ss, recv_sem=rs, device_id=device, device_id_type=MESH
        )

    barrier = pltpu.get_barrier_semaphore()
    for k in range(1, 4):
        pl.semaphore_signal(barrier, inc=1, device_id={"row": row_at(0, k)}, device_id_type=MESH)
        pl.semaphore_signal(barrier, inc=1, device_id={"row": row_at(k, 0)}, device_id_type=MESH)
        pl.semaphore_signal(barrier, inc=1, device_id=x_peer(k), device_id_type=MESH)
    pl.semaphore_signal(barrier, inc=1, device_id=core_peer, device_id_type=MESH)
    pl.semaphore_signal(barrier, inc=1, device_id=zh_peer, device_id_type=MESH)

    small = []
    for k, (src, dst) in enumerate(((sub_h, sub_s), (rp_h, rp_s), (lp_h, lp_s), (sq_h, sq_v))):
        cp = pltpu.make_async_copy(src, dst, ssem.at[k])
        cp.start()
        small.append(cp)
    win_copies = []
    for w in range(16):
        cp = pltpu.make_async_copy(win_h.at[:, pl.ds(w * BS, BS)], win_v.at[w], wsem.at[w])
        cp.start()
        win_copies.append(cp)
    left_copies = []
    for part in range(4):
        cp = pltpu.make_async_copy(
            left_h.at[pl.ds(part * 4096, 4096)], left_v.at[pl.ds(part * 4096, 4096)], lsem.at[1 + part]
        )
        cp.start()
        left_copies.append(cp)
    for cp in small:
        cp.wait()

    lane = lax.broadcasted_iota(jnp.int32, (8, 128), 1)
    mine = jnp.zeros((8, 128), jnp.int32)
    for w in range(NW):
        mine = jnp.where(lane == y * NW + w, rp_s[0, sub_s[w]], mine)
    py_v[y] = mine
    for cp in win_copies:
        cp.wait()
    for w in range(NW):
        block = win_v[sub_s[w]].T
        for h in range(NH):
            for to in range(4):
                at = 32 * h + 8 * to
                spread[h, to, w] = block[at:at + 8, :]
    pl.semaphore_wait(barrier, 11)

    pt = []
    for dy in (1, 3, 2):
        cp = remote(py_v.at[y], py_v.at[y], py_ss.at[dy], py_rs.at[dy], {"row": row_at(0, dy)})
        cp.start()
        pt.append(cp)

    a2a = []
    for h in range(NH):
        row = []
        for dy in (1, 3, 2):
            to = lax.rem(y + dy, 4)
            cp = remote(spread.at[h, to], rec[h].at[pl.ds(y * NW, NW)], a_ss.at[h, dy], a_rs.at[h, dy], {"row": row_at(0, dy)})
            cp.start()
            row.append(cp)
        a2a.append(row)
        rec[h][pl.ds(y * NW, NW)] = spread[h, y]

    def prepare():
        for cp in left_copies:
            cp.wait()

        def body(piece, _):
            at = lax.rem(piece, 2) * 512 + lax.rem(piece // 2, 2) * 256 + (piece // 4) * 64
            at = pl.multiple_of(at, 64)
            for q in range(NR):
                v = left_v[pl.ds(piece * 1024 + q, 64, stride=16), :]
                v = jnp.where(jnp.full((64, 128), lp_s[piece // 2, q], jnp.int32) != 0, v, 0.0)
                hi = v.astype(jnp.bfloat16)
                ahi[pl.ds(at, 64), q * BS:(q + 1) * BS] = hi
                alo[pl.ds(at, 64), q * BS:(q + 1) * BS] = (v - hi.astype(jnp.float32)).astype(jnp.bfloat16)
            return 0

        lax.fori_loop(0, 16, body, 0)

    def column(v):
        return jnp.broadcast_to(v[0:1, :], (128, 128)).T

    for cp in pt:
        cp.wait_recv()
    pool = (py_v[0] + py_v[1]) + (py_v[2] + py_v[3])
    pz_v[z] = pool
    for dz in (1, 3, 2):
        cp = remote(pz_v.at[z], pz_v.at[z], pz_ss.at[dz], pz_rs.at[dz], {"row": row_at(dz, 0)})
        cp.start()
        pt.append(cp)
    upto = pool
    for s in (1, 2, 4, 8, 16):
        upto = upto + jnp.where(lane >= s, pltpu.roll(upto, s, 1), 0)
    blk = lax.broadcasted_iota(jnp.int32, (32, 128), 0)
    slot = lax.broadcasted_iota(jnp.int32, (32, 128), 1)
    first = jnp.where((column(pool)[0:32, :] != 0) & (column(upto - pool)[0:32, :] == slot), blk, 0)
    one_v[...] = jnp.broadcast_to(jnp.sum(first, axis=0, keepdims=True), (8, 128))
    to_one = pltpu.make_async_copy(one_v, one_s, lsem.at[0])
    to_one.start()
    to_one.wait()

    zg = []
    for h in range(NH):
        for cp in a2a[h]:
            cp.wait_recv()

        def pack(j, _, h=h):
            at = one_s[0, j]
            zr[h][z * cz + j] = rec[h][at]
            return 0

        if cz <= 20:
            for j in range(cz):
                pack(j, 0)
        else:
            lax.fori_loop(0, cz, pack, 0)
        row = {}
        part = zr[h].at[pl.ds(z * cz, cz)]
        for dz in (2, 1, 3):
            row[dz] = remote(part, part, z_ss.at[h, dz], z_rs.at[h, dz], {"row": row_at(dz, 0)})
        row[2].start()

        @pl.when(z != 3)
        def _(cp=row[1]):
            cp.start()

        @pl.when(z != 0)
        def _(cp=row[3]):
            cp.start()

        zg.append(row)

    for cp in pt[3:]:
        cp.wait_recv()
    pat = jnp.where(lane < 32, pz_v[0], 0)
    for k in range(1, 4):
        pat = jnp.where(lane // 32 == k, pltpu.roll(pz_v[k], 32 * k, 1), pat)
    in_pool = lax.rem(lane, 32)
    c32 = pat
    for s in (1, 2, 4, 8, 16):
        c32 = c32 + jnp.where(in_pool >= s, pltpu.roll(c32, s, 1), 0)
    call = pat
    for s in (1, 2, 4, 8, 16, 32, 64):
        call = call + jnp.where(lane >= s, pltpu.roll(call, s, 1), 0)
    rank = call - pat
    zsrc = (lane // 32) * cz + jnp.minimum(c32 - pat, cz - 1)
    slot = lax.broadcasted_iota(jnp.int32, (128, 128), 1)
    second = jnp.where((column(pat) != 0) & (column(rank) == slot), column(zsrc), 0)
    idx_v[0:2, :] = pat[0:2, :]
    idx_v[1:2, :] = jnp.sum(second, axis=0, keepdims=True)
    idx_v[2:3, :] = jnp.minimum(rank, cy - 1)[0:1, :]
    idx_v[3:4, :] = pat[0:1, :]
    idx_v[4:8, :] = pat[0:4, :]
    over = jnp.where((in_pool == 31) & (c32 > cz), 1, 0) + jnp.where((lane == 127) & (call > cy), 1, 0)
    for s in (1, 2, 4, 8, 16, 32, 64):
        over = over + pltpu.roll(over, s, 1)
    fl_a[...] = over
    to_s = pltpu.make_async_copy(idx_v, idx_s, lsem.at[5])
    to_s.start()
    to_s.wait()

    zf = []
    for h in range(NH):
        up = zr[h].at[pl.ds(0, cz)]
        down = zr[h].at[pl.ds(3 * cz, cz)]
        zf.append((
            remote(up, up, z_ss.at[h, 0], z_rs.at[h, 3], {"row": 12 + y}),
            remote(down, down, z_ss.at[h, 0], z_rs.at[h, 1], {"row": y}),
        ))

    def z_forward(h):
        zg[h][2].wait_recv()

        @pl.when(z == 2)
        def _():
            zf[h][0].start()

        @pl.when(z == 1)
        def _():
            zf[h][1].start()

    sides = ((0, 1), (1, 3))

    def yg(h, side, k):
        part = yr[h].at[y, pl.ds(k * half, half)]
        return remote(part, part, y_ss.at[h, side, k], y_rs.at[h, side, k], {"row": row_at(0, sides[side][1])})

    def fg(h, side):
        part = yr[h].at[lax.rem(y + (3 if side == 0 else 1), 4), pl.ds(side * half, half)]
        return remote(part, part, f_ss.at[h, side], f_rs.at[h, side], {"row": row_at(0, sides[side][1])})

    def y_send(h):
        zg[h][1].wait_recv()
        zg[h][3].wait_recv()

        def pack(j, _):
            at = idx_s[1, j]
            yr[h][y, j] = zr[h][at]
            return 0

        if cy <= 64:
            def ten(i, _):
                for k in range(10):
                    pack(i * 10 + k, 0)
                return 0

            lax.fori_loop(0, cy // 10, ten, 0)
        else:
            lax.fori_loop(0, cy, pack, 0)
        for side in (0, 1):
            for k in ((0, 1) if side == 0 else (1, 0)):
                yg(h, side, k).start()

    def y_forward(h):
        for side in (0, 1):
            yg(h, side, side).wait_recv()
            fg(h, side).start()

    def y_wait(h):
        for side in (0, 1):
            yg(h, side, 1 - side).wait_recv()
            fg(h, side).wait_recv()

    def expand(h):
        def body(w, _):
            at = pl.multiple_of(w * 32, 32)
            for q in range(NR):
                place = idx_s[2, q * NW + w]
                keep = jnp.full((32, 128), idx_s[3, q * NW + w], jnp.int32) != 0
                v = jnp.concatenate([yr[h][k, place] for k in range(4)], axis=0)
                v = jnp.where(keep, v, 0.0)
                hi = v.astype(jnp.bfloat16)
                bhi[pl.ds(at, 32), q * BS:(q + 1) * BS] = hi
                blo[pl.ds(at, 32), q * BS:(q + 1) * BS] = (v - hi.astype(jnp.float32)).astype(jnp.bfloat16)
            return 0

        lax.fori_loop(0, NW, body, 0)

    def product(s):
        swap_core = 1 - lax.rem(s, 2)
        swap_zh = 1 - lax.rem(s // 2, 2)
        core_to = core + swap_core * (1 - 2 * core)
        zh_to = zh + swap_zh * (1 - 2 * zh)
        at = pl.multiple_of(core_to * 512 + zh_to * 256, 256)
        a_hi, a_lo = ahi[pl.ds(at, 256), :], alo[pl.ds(at, 256), :]
        b_hi, b_lo = bhi[...], blo[...]
        return dot_nt(a_hi, b_hi) + dot_nt(a_hi, b_lo) + dot_nt(a_lo, b_hi)

    def cg(h, p):
        return remote(prod.at[4 * h + 2 * p], cr.at[h, p], c_ss.at[h, p], c_rs.at[h, p], core_peer)

    def xg(h, p, dx):
        part = prod.at[4 * h + 2 * p + 1, pl.ds(pl.multiple_of(lax.rem(x + dx, 4) * 64, 64), 64)]
        return remote(part, xr.at[h, p, dx - 1], x_ss.at[h, p, dx], x_rs.at[h, p, dx], x_peer(dx))

    def vg(h):
        return remote(vz.at[h, 0], zx.at[h], v_ss.at[h], v_rs.at[h], zh_peer)

    def flg(k):
        if k == 0:
            return remote(fl_a, fl_c, fl_ss.at[0], fl_rs.at[0], core_peer)
        if k == 4:
            return remote(fl_b.at[1], fl_z, fl_ss.at[4], fl_rs.at[4], zh_peer)
        return remote(fl_b.at[0], fl_x.at[k - 1], fl_ss.at[k], fl_rs.at[k], x_peer(k))

    def to_core(h, p):
        cg(h, p).start()
        if (h, p) == (0, 0):
            flg(0).start()

    def over_x(h, p):
        cg(h, p).wait_recv()
        prod[4 * h + 2 * p + 1] = prod[4 * h + 2 * p + 1] + cr[h, p]
        for dx in (2, 1, 3):
            xg(h, p, dx).start()
        if (h, p) == (0, 0):
            flg(0).wait_recv()
            fl_b[0] = fl_a[...] + fl_c[...]
            for dx in (1, 3, 2):
                flg(dx).start()

    def sum_x(h, p):
        total = prod[4 * h + 2 * p + 1, pl.ds(pl.multiple_of(x * 64, 64), 64), :]
        for dx in (1, 3, 2):
            xg(h, p, dx).wait_recv()
            total = total + xr[h, p, dx - 1]
        vz[h, p] = total

    def over_zh(h):
        sum_x(h, 0)
        vg(h).start()
        if h == 0:
            for dx in (1, 3, 2):
                flg(dx).wait_recv()
            fl_b[1] = (fl_b[0] + fl_x[0]) + (fl_x[1] + fl_x[2])
            flg(4).start()

    lane64 = lax.broadcasted_iota(jnp.int32, (64, 128), 1)

    def finish(h):
        vg(h).wait_recv()
        total = vz[h, 1] + zx[h]
        for w in range(NW):
            tile = total[:, (w // 4) * 128:(w // 4 + 1) * 128]
            shift = (32 * h - 32 * (w % 4)) % 128
            if shift:
                tile = pltpu.roll(tile, shift, 1)
            cols = slice(w * BS, (w + 1) * BS)
            value = 3.0 * sq_v[:, cols] - 2.0 * tile
            if h:
                value = jnp.where(lane64 // 32 == h, value, out_v[:, cols])
            out_v[:, cols] = value
        if h == 0:
            flg(4).wait_recv()
            one_v[...] = fl_b[1] + fl_z[...]
            to_flag = pltpu.make_async_copy(one_v, one_s, lsem.at[0])
            to_flag.start()
            to_flag.wait()
            flag_s[0, 0] = one_s[0, 0]

    prepare()
    z_forward(0)
    y_send(0)
    z_forward(1)
    y_forward(0)
    y_send(1)

    def step(s, _):
        for h in range(NH):
            @pl.when(s == 4 * h)
            def _(h=h):
                y_wait(h)
                expand(h)

        prod[s] = product(s)

        for h in range(NH):
            @pl.when(s == 4 * h)
            def _(h=h):
                to_core(h, 0)
                if h + 1 < NH:
                    y_forward(h + 1)
                if h + 2 < NH:
                    z_forward(h + 2)
                    y_send(h + 2)

            @pl.when(s == 4 * h + 1)
            def _(h=h):
                over_x(h, 0)

            @pl.when(s == 4 * h + 2)
            def _(h=h):
                to_core(h, 1)
                if h >= 1:
                    over_zh(h - 1)

            @pl.when(s == 4 * h + 3)
            def _(h=h):
                if h >= 1:
                    sum_x(h - 1, 1)
                over_x(h, 1)
                if h >= 2:
                    finish(h - 2)

        return 0

    lax.fori_loop(0, 4 * NH, step, 0)
    over_zh(NH - 1)
    sum_x(NH - 1, 1)
    finish(NH - 2)
    finish(NH - 1)

    for cp in pt:
        cp.wait_send()
    for row in a2a:
        for cp in row:
            cp.wait_send()
    for row in zg:
        row[2].wait_send()

    @pl.when(z != 3)
    def _():
        for row in zg:
            row[1].wait_send()

    @pl.when(z != 0)
    def _():
        for row in zg:
            row[3].wait_send()

    @pl.when(z == 2)
    def _():
        for row in zf:
            row[0].wait_send()

    @pl.when(z == 1)
    def _():
        for row in zf:
            row[1].wait_send()

    for h in range(NH):
        for side in (0, 1):
            fg(h, side).wait_send()
            for k in (0, 1):
                yg(h, side, k).wait_send()
        for p in (0, 1):
            cg(h, p).wait_send()
            for dx in (1, 2, 3):
                xg(h, p, dx).wait_send()
        vg(h).wait_send()
    for k in range(5):
        flg(k).wait_send()


def run(cz, cy, collective_id, left, lp, win, rp, sub, sq):
    any_ = pl.BlockSpec(memory_space=pl.ANY)
    vmem = pl.BlockSpec(memory_space=pltpu.VMEM)
    smem = pl.BlockSpec(memory_space=pltpu.SMEM)
    f32, bf16, i32 = jnp.float32, jnp.bfloat16, jnp.int32
    dma = pltpu.SemaphoreType.DMA
    scratch = [
        pltpu.SMEM((8, NR), i32),
        pltpu.SMEM((1, 16), i32),
        pltpu.SMEM((8,), i32),
        pltpu.VMEM((64, 1024), f32),
        pltpu.VMEM((16384, 128), f32),
        pltpu.VMEM((16, 128, 128), f32),
        pltpu.VMEM((1024, 2048), bf16),
        pltpu.VMEM((1024, 2048), bf16),
        pltpu.VMEM((NH, 4, NW, 8, 128), f32),
        pltpu.VMEM((4, 8, 128), i32),
        pltpu.VMEM((4, 8, 128), i32),
        pltpu.VMEM((8, 128), i32),
        pltpu.SMEM((8, 128), i32),
        pltpu.VMEM((8, 128), i32),
        pltpu.SMEM((8, 128), i32),
        pltpu.VMEM((256, 2048), bf16),
        pltpu.VMEM((256, 2048), bf16),
        pltpu.VMEM((4 * NH, 256, 256), f32),
        pltpu.VMEM((NH, 2, 256, 256), f32),
        pltpu.VMEM((NH, 2, 3, 64, 256), f32),
        pltpu.VMEM((NH, 2, 64, 256), f32),
        pltpu.VMEM((NH, 64, 256), f32),
        pltpu.VMEM((8, 128), i32),
        pltpu.VMEM((2, 8, 128), i32),
        pltpu.VMEM((8, 128), i32),
        pltpu.VMEM((3, 8, 128), i32),
        pltpu.VMEM((8, 128), i32),
    ]
    scratch += [pltpu.VMEM((4 * NW, 8, 128), f32) for _ in range(NH)]
    scratch += [pltpu.VMEM((4 * cz, 8, 128), f32) for _ in range(NH)]
    scratch += [pltpu.VMEM((4, cy, 8, 128), f32) for _ in range(NH)]
    scratch += [
        dma((4,)), dma((16,)), dma((6,)),
        dma((4,)), dma((4,)), dma((4,)), dma((4,)),
        dma((NH, 4)), dma((NH, 4)),
        dma((NH, 4)), dma((NH, 4)),
        dma((NH, 2, 2)), dma((NH, 2, 2)),
        dma((NH, 2)), dma((NH, 2)),
        dma((NH, 2)), dma((NH, 2)),
        dma((NH, 2, 4)), dma((NH, 2, 4)),
        dma((NH,)), dma((NH,)),
        dma((5,)), dma((5,)),
    ]
    return pl.pallas_call(
        functools.partial(kernel, cz, cy),
        out_shape=(jax.ShapeDtypeStruct((64, 1024), f32), jax.ShapeDtypeStruct((1, 1), i32)),
        in_specs=[any_] * 6,
        out_specs=(vmem, smem),
        scratch_shapes=scratch,
        compiler_params=pltpu.CompilerParams(
            collective_id=collective_id, has_side_effects=True, vmem_limit_bytes=56 * 2**20
        ),
    )(left, lp, win, rp, sub, sq)


def shards(left_blocks, left_pattern, right_window, right_pattern, subset_cols, square_cols):
    args = (
        left_blocks.reshape(1024 * NR, BS),
        left_pattern.reshape(8, NR),
        right_window.reshape(128, 2048),
        right_pattern.reshape(1, 16),
        subset_cols,
        square_cols,
    )
    fast, flag = run(18, 50, 0, *args)
    return lax.cond(
        flag[0, 0] > 0,
        lambda value, *rest: run(32, 128, 1, *rest)[0],
        lambda value, *rest: value,
        fast, *args,
    )


def solution(mesh):
    return jax.shard_map(
        shards,
        mesh=mesh,
        in_specs=(
            P("row", ("col", "depth"), None),
            P("row", ("col", "depth"), None),
            P(("col", "depth"), "row", None),
            P(("col", "depth"), "row", None),
            P(),
            P(("row", "col", "depth"), None),
        ),
        out_specs=P(("row", "col", "depth"), None),
        check_vma=False,
    )
```

```python
import functools

import jax
import jax.numpy as jnp
from jax import lax
from jax.experimental import pallas as pl
from jax.experimental.pallas import tpu as pltpu
from jax.sharding import PartitionSpec as P

MESH = pl.DeviceIdType.MESH
BS = 128
NH = 4
NW = 8
NR = 16


def dot_nt(a, b):
    return lax.dot_general(a, b, (((1,), (1,)), ((), ())), preferred_element_type=jnp.float32)


def kernel(cz, cy, left_h, lp_h, win_h, rp_h, sub_h, sq_h, out_v, flag_s, *scratch):
    (lp_s, rp_s, sub_s, sq_v, left_v, win_v, ahi, alo, spread, py_v, pz_v, one_v, one_s, idx_v, idx_s, bhi, blo,
     prod, cr, xr, vz, zx, fl_a, fl_b, fl_c, fl_x, fl_z,
     rec0, rec1, rec2, rec3, zr0, zr1, zr2, zr3, yr0, yr1, yr2, yr3,
     ssem, wsem, lsem, py_ss, py_rs, pz_ss, pz_rs, a_ss, a_rs, z_ss, z_rs, y_ss, y_rs, f_ss, f_rs,
     c_ss, c_rs, x_ss, x_rs, v_ss, v_rs, fl_ss, fl_rs) = scratch
    rec = (rec0, rec1, rec2, rec3)
    zr = (zr0, zr1, zr2, zr3)
    yr = (yr0, yr1, yr2, yr3)
    half = cy // 2

    r = lax.axis_index("row")
    x = lax.axis_index("col")
    d = lax.axis_index("depth")
    y = lax.rem(r, 4)
    z = r // 4
    core = lax.rem(d, 2)
    zh = d // 2

    def row_at(dz, dy):
        return lax.rem(z + dz, 4) * 4 + lax.rem(y + dy, 4)

    core_peer = {"depth": d + 1 - 2 * core}
    zh_peer = {"depth": lax.rem(d + 2, 4)}

    def x_peer(dx):
        return {"col": lax.rem(x + dx, 4)}

    def remote(src, dst, ss, rs, device):
        return pltpu.make_async_remote_copy(
            src_ref=src, dst_ref=dst, send_sem=ss, recv_sem=rs, device_id=device, device_id_type=MESH
        )

    barrier = pltpu.get_barrier_semaphore()
    for k in range(1, 4):
        pl.semaphore_signal(barrier, inc=1, device_id={"row": row_at(0, k)}, device_id_type=MESH)
        pl.semaphore_signal(barrier, inc=1, device_id={"row": row_at(k, 0)}, device_id_type=MESH)
        pl.semaphore_signal(barrier, inc=1, device_id=x_peer(k), device_id_type=MESH)
    pl.semaphore_signal(barrier, inc=1, device_id=core_peer, device_id_type=MESH)
    pl.semaphore_signal(barrier, inc=1, device_id=zh_peer, device_id_type=MESH)

    small = []
    for k, (src, dst) in enumerate(((sub_h, sub_s), (rp_h, rp_s), (lp_h, lp_s), (sq_h, sq_v))):
        cp = pltpu.make_async_copy(src, dst, ssem.at[k])
        cp.start()
        small.append(cp)
    win_copies = []
    for w in range(16):
        cp = pltpu.make_async_copy(win_h.at[:, pl.ds(w * BS, BS)], win_v.at[w], wsem.at[w])
        cp.start()
        win_copies.append(cp)
    left_copies = []
    for part in range(4):
        cp = pltpu.make_async_copy(
            left_h.at[pl.ds(part * 4096, 4096)], left_v.at[pl.ds(part * 4096, 4096)], lsem.at[1 + part]
        )
        cp.start()
        left_copies.append(cp)
    for cp in small:
        cp.wait()

    lane = lax.broadcasted_iota(jnp.int32, (8, 128), 1)
    mine = jnp.zeros((8, 128), jnp.int32)
    for w in range(NW):
        mine = jnp.where(lane == y * NW + w, rp_s[0, sub_s[w]], mine)
    py_v[y] = mine
    for cp in win_copies:
        cp.wait()
    for w in range(NW):
        block = win_v[sub_s[w]].T
        for h in range(NH):
            for to in range(4):
                at = 32 * h + 8 * to
                spread[h, to, w] = block[at:at + 8, :]
    pl.semaphore_wait(barrier, 11)

    pt = []
    for dy in (1, 3, 2):
        cp = remote(py_v.at[y], py_v.at[y], py_ss.at[dy], py_rs.at[dy], {"row": row_at(0, dy)})
        cp.start()
        pt.append(cp)

    a2a = []
    for h in range(NH):
        row = []
        for dy in (1, 3, 2):
            to = lax.rem(y + dy, 4)
            cp = remote(spread.at[h, to], rec[h].at[pl.ds(y * NW, NW)], a_ss.at[h, dy], a_rs.at[h, dy], {"row": row_at(0, dy)})
            cp.start()
            row.append(cp)
        a2a.append(row)
        rec[h][pl.ds(y * NW, NW)] = spread[h, y]

    def prepare(first):
        for cp in left_copies[first // 4:first // 4 + 2]:
            cp.wait()

        def body(piece, _):
            at = lax.rem(piece, 2) * 512 + lax.rem(piece // 2, 2) * 256 + (piece // 4) * 64
            at = pl.multiple_of(at, 64)
            for q in range(NR):
                v = left_v[pl.ds(piece * 1024 + q, 64, stride=16), :]
                v = jnp.where(jnp.full((64, 128), lp_s[piece // 2, q], jnp.int32) != 0, v, 0.0)
                hi = v.astype(jnp.bfloat16)
                ahi[pl.ds(at, 64), q * BS:(q + 1) * BS] = hi
                alo[pl.ds(at, 64), q * BS:(q + 1) * BS] = (v - hi.astype(jnp.float32)).astype(jnp.bfloat16)
            return 0

        lax.fori_loop(first, first + 8, body, 0)

    def column(v):
        return jnp.broadcast_to(v[0:1, :], (128, 128)).T

    for cp in pt:
        cp.wait_recv()
    pool = (py_v[0] + py_v[1]) + (py_v[2] + py_v[3])
    pz_v[z] = pool
    for dz in (1, 3, 2):
        cp = remote(pz_v.at[z], pz_v.at[z], pz_ss.at[dz], pz_rs.at[dz], {"row": row_at(dz, 0)})
        cp.start()
        pt.append(cp)
    upto = pool
    for s in (1, 2, 4, 8, 16):
        upto = upto + jnp.where(lane >= s, pltpu.roll(upto, s, 1), 0)
    blk = lax.broadcasted_iota(jnp.int32, (32, 128), 0)
    slot = lax.broadcasted_iota(jnp.int32, (32, 128), 1)
    place = jnp.where(pool != 0, upto - pool, 255)
    first = jnp.where(column(place)[0:32, :] == slot, blk, 0)
    one_v[...] = jnp.broadcast_to(jnp.sum(first, axis=0, keepdims=True), (8, 128))
    to_one = pltpu.make_async_copy(one_v, one_s, lsem.at[0])
    to_one.start()
    to_one.wait()

    zg = []
    for h in range(NH):
        for cp in a2a[h]:
            cp.wait_recv()

        def pack(j, _, h=h):
            at = one_s[0, j]
            zr[h][z * cz + j] = rec[h][at]
            return 0

        if cz <= 20:
            for j in range(cz):
                pack(j, 0)
        else:
            lax.fori_loop(0, cz, pack, 0)
        row = {}
        part = zr[h].at[pl.ds(z * cz, cz)]
        for dz in (2, 1, 3):
            row[dz] = remote(part, part, z_ss.at[h, dz], z_rs.at[h, dz], {"row": row_at(dz, 0)})
        row[2].start()

        @pl.when(z != 3)
        def _(cp=row[1]):
            cp.start()

        @pl.when(z != 0)
        def _(cp=row[3]):
            cp.start()

        zg.append(row)

    for cp in pt[3:]:
        cp.wait_recv()
    pat = jnp.where(lane < 32, pz_v[0], 0)
    for k in range(1, 4):
        pat = jnp.where(lane // 32 == k, pltpu.roll(pz_v[k], 32 * k, 1), pat)
    in_pool = lax.rem(lane, 32)
    c32 = pat
    for s in (1, 2, 4, 8, 16):
        c32 = c32 + jnp.where(in_pool >= s, pltpu.roll(c32, s, 1), 0)
    call = pat
    for s in (1, 2, 4, 8, 16, 32, 64):
        call = call + jnp.where(lane >= s, pltpu.roll(call, s, 1), 0)
    rank = call - pat
    zsrc = (lane // 32) * cz + jnp.minimum(c32 - pat, cz - 1)
    slot = lax.broadcasted_iota(jnp.int32, (128, 128), 1)
    second = jnp.where(column(jnp.where(pat != 0, rank, 255)) == slot, column(zsrc), 0)
    idx_v[0:2, :] = pat[0:2, :]
    idx_v[1:2, :] = jnp.sum(second, axis=0, keepdims=True)
    idx_v[2:3, :] = jnp.minimum(rank, cy - 1)[0:1, :]
    idx_v[3:4, :] = pat[0:1, :]
    idx_v[4:8, :] = pat[0:4, :]
    over = jnp.where((in_pool == 31) & (c32 > cz), 1, 0) + jnp.where((lane == 127) & (call > cy), 1, 0)
    for s in (1, 2, 4, 8, 16, 32, 64):
        over = over + pltpu.roll(over, s, 1)
    fl_a[...] = over
    to_s = pltpu.make_async_copy(idx_v, idx_s, lsem.at[5])
    to_s.start()
    to_s.wait()

    zf = []
    for h in range(NH):
        up = zr[h].at[pl.ds(0, cz)]
        down = zr[h].at[pl.ds(3 * cz, cz)]
        zf.append((
            remote(up, up, z_ss.at[h, 0], z_rs.at[h, 3], {"row": 12 + y}),
            remote(down, down, z_ss.at[h, 0], z_rs.at[h, 1], {"row": y}),
        ))

    def z_forward(h):
        zg[h][2].wait_recv()

        @pl.when(z == 2)
        def _():
            zf[h][0].start()

        @pl.when(z == 1)
        def _():
            zf[h][1].start()

    sides = ((0, 1), (1, 3))

    def yg(h, side, k):
        part = yr[h].at[y, pl.ds(k * half, half)]
        return remote(part, part, y_ss.at[h, side, k], y_rs.at[h, side, k], {"row": row_at(0, sides[side][1])})

    def fg(h, side):
        part = yr[h].at[lax.rem(y + (3 if side == 0 else 1), 4), pl.ds(side * half, half)]
        return remote(part, part, f_ss.at[h, side], f_rs.at[h, side], {"row": row_at(0, sides[side][1])})

    def y_send(h):
        zg[h][1].wait_recv()
        zg[h][3].wait_recv()

        def pack(j, _):
            at = idx_s[1, j]
            yr[h][y, j] = zr[h][at]
            return 0

        if cy <= 64:
            def ten(i, _):
                for k in range(10):
                    pack(i * 10 + k, 0)
                return 0

            lax.fori_loop(0, cy // 10, ten, 0)
        else:
            lax.fori_loop(0, cy, pack, 0)
        for side in (0, 1):
            for k in ((0, 1) if side == 0 else (1, 0)):
                yg(h, side, k).start()

    def y_forward(h):
        for side in (0, 1):
            yg(h, side, side).wait_recv()
            fg(h, side).start()

    def y_wait(h):
        for side in (0, 1):
            yg(h, side, 1 - side).wait_recv()
            fg(h, side).wait_recv()

    def expand(h):
        def body(w, _):
            at = pl.multiple_of(w * 32, 32)
            for q in range(NR):
                place = idx_s[2, q * NW + w]
                keep = jnp.full((32, 128), idx_s[3, q * NW + w], jnp.int32) != 0
                v = jnp.concatenate([yr[h][k, place] for k in range(4)], axis=0)
                v = jnp.where(keep, v, 0.0)
                hi = v.astype(jnp.bfloat16)
                bhi[pl.ds(at, 32), q * BS:(q + 1) * BS] = hi
                blo[pl.ds(at, 32), q * BS:(q + 1) * BS] = (v - hi.astype(jnp.float32)).astype(jnp.bfloat16)
            return 0

        lax.fori_loop(0, NW, body, 0)

    def product(s):
        swap_core = 1 - lax.rem(s, 2)
        swap_zh = 1 - lax.rem(s // 2, 2)
        core_to = core + swap_core * (1 - 2 * core)
        zh_to = zh + swap_zh * (1 - 2 * zh)
        at = pl.multiple_of(core_to * 512 + zh_to * 256, 256)
        a_hi, a_lo = ahi[pl.ds(at, 256), :], alo[pl.ds(at, 256), :]
        b_hi, b_lo = bhi[...], blo[...]
        return dot_nt(a_hi, b_hi) + dot_nt(a_hi, b_lo) + dot_nt(a_lo, b_hi)

    def cg(h, p):
        return remote(prod.at[4 * h + 2 * p], cr.at[h, p], c_ss.at[h, p], c_rs.at[h, p], core_peer)

    def xg(h, p, dx):
        part = prod.at[4 * h + 2 * p + 1, pl.ds(pl.multiple_of(lax.rem(x + dx, 4) * 64, 64), 64)]
        return remote(part, xr.at[h, p, dx - 1], x_ss.at[h, p, dx], x_rs.at[h, p, dx], x_peer(dx))

    def vg(h):
        return remote(vz.at[h, 0], zx.at[h], v_ss.at[h], v_rs.at[h], zh_peer)

    def flg(k):
        if k == 0:
            return remote(fl_a, fl_c, fl_ss.at[0], fl_rs.at[0], core_peer)
        if k == 4:
            return remote(fl_b.at[1], fl_z, fl_ss.at[4], fl_rs.at[4], zh_peer)
        return remote(fl_b.at[0], fl_x.at[k - 1], fl_ss.at[k], fl_rs.at[k], x_peer(k))

    def to_core(h, p):
        cg(h, p).start()
        if (h, p) == (0, 0):
            flg(0).start()

    def over_x(h, p):
        cg(h, p).wait_recv()
        prod[4 * h + 2 * p + 1] = prod[4 * h + 2 * p + 1] + cr[h, p]
        for dx in (2, 1, 3):
            xg(h, p, dx).start()
        if (h, p) == (0, 0):
            flg(0).wait_recv()
            fl_b[0] = fl_a[...] + fl_c[...]
            for dx in (1, 3, 2):
                flg(dx).start()

    def sum_x(h, p):
        total = prod[4 * h + 2 * p + 1, pl.ds(pl.multiple_of(x * 64, 64), 64), :]
        for dx in (1, 3, 2):
            xg(h, p, dx).wait_recv()
            total = total + xr[h, p, dx - 1]
        vz[h, p] = total

    def over_zh(h):
        sum_x(h, 0)
        vg(h).start()
        if h == 0:
            for dx in (1, 3, 2):
                flg(dx).wait_recv()
            fl_b[1] = (fl_b[0] + fl_x[0]) + (fl_x[1] + fl_x[2])
            flg(4).start()

    lane64 = lax.broadcasted_iota(jnp.int32, (64, 128), 1)

    def finish(h):
        vg(h).wait_recv()
        total = vz[h, 1] + zx[h]
        for w in range(NW):
            tile = total[:, (w // 4) * 128:(w // 4 + 1) * 128]
            shift = (32 * h - 32 * (w % 4)) % 128
            if shift:
                tile = pltpu.roll(tile, shift, 1)
            cols = slice(w * BS, (w + 1) * BS)
            value = 3.0 * sq_v[:, cols] - 2.0 * tile
            if h:
                value = jnp.where(lane64 // 32 == h, value, out_v[:, cols])
            out_v[:, cols] = value
        if h == 0:
            flg(4).wait_recv()
            one_v[...] = fl_b[1] + fl_z[...]
            to_flag = pltpu.make_async_copy(one_v, one_s, lsem.at[0])
            to_flag.start()
            to_flag.wait()
            flag_s[0, 0] = one_s[0, 0]

    prepare(0)
    z_forward(0)
    y_send(0)
    prepare(8)
    z_forward(1)
    y_forward(0)
    y_send(1)

    def step(s, _):
        for h in range(NH):
            @pl.when(s == 4 * h)
            def _(h=h):
                y_wait(h)
                expand(h)

        prod[s] = product(s)

        for h in range(NH):
            @pl.when(s == 4 * h)
            def _(h=h):
                to_core(h, 0)
                if h + 1 < NH:
                    y_forward(h + 1)
                if h + 2 < NH:
                    z_forward(h + 2)
                    y_send(h + 2)

            @pl.when(s == 4 * h + 1)
            def _(h=h):
                over_x(h, 0)

            @pl.when(s == 4 * h + 2)
            def _(h=h):
                to_core(h, 1)
                if h >= 1:
                    over_zh(h - 1)

            @pl.when(s == 4 * h + 3)
            def _(h=h):
                if h + 1 < NH:
                    if h >= 1:
                        sum_x(h - 1, 1)
                    over_x(h, 1)
                    if h >= 2:
                        finish(h - 2)

        return 0

    lax.fori_loop(0, 4 * NH, step, 0)
    over_x(NH - 1, 1)
    over_zh(NH - 1)
    sum_x(NH - 2, 1)
    finish(NH - 3)
    finish(NH - 2)
    sum_x(NH - 1, 1)
    finish(NH - 1)

    for cp in pt:
        cp.wait_send()
    for row in a2a:
        for cp in row:
            cp.wait_send()
    for row in zg:
        row[2].wait_send()

    @pl.when(z != 3)
    def _():
        for row in zg:
            row[1].wait_send()

    @pl.when(z != 0)
    def _():
        for row in zg:
            row[3].wait_send()

    @pl.when(z == 2)
    def _():
        for row in zf:
            row[0].wait_send()

    @pl.when(z == 1)
    def _():
        for row in zf:
            row[1].wait_send()

    for h in range(NH):
        for side in (0, 1):
            fg(h, side).wait_send()
            for k in (0, 1):
                yg(h, side, k).wait_send()
        for p in (0, 1):
            cg(h, p).wait_send()
            for dx in (1, 2, 3):
                xg(h, p, dx).wait_send()
        vg(h).wait_send()
    for k in range(5):
        flg(k).wait_send()


def run(cz, cy, collective_id, left, lp, win, rp, sub, sq):
    any_ = pl.BlockSpec(memory_space=pl.ANY)
    vmem = pl.BlockSpec(memory_space=pltpu.VMEM)
    smem = pl.BlockSpec(memory_space=pltpu.SMEM)
    f32, bf16, i32 = jnp.float32, jnp.bfloat16, jnp.int32
    dma = pltpu.SemaphoreType.DMA
    scratch = [
        pltpu.SMEM((8, NR), i32),
        pltpu.SMEM((1, 16), i32),
        pltpu.SMEM((8,), i32),
        pltpu.VMEM((64, 1024), f32),
        pltpu.VMEM((16384, 128), f32),
        pltpu.VMEM((16, 128, 128), f32),
        pltpu.VMEM((1024, 2048), bf16),
        pltpu.VMEM((1024, 2048), bf16),
        pltpu.VMEM((NH, 4, NW, 8, 128), f32),
        pltpu.VMEM((4, 8, 128), i32),
        pltpu.VMEM((4, 8, 128), i32),
        pltpu.VMEM((8, 128), i32),
        pltpu.SMEM((8, 128), i32),
        pltpu.VMEM((8, 128), i32),
        pltpu.SMEM((8, 128), i32),
        pltpu.VMEM((256, 2048), bf16),
        pltpu.VMEM((256, 2048), bf16),
        pltpu.VMEM((4 * NH, 256, 256), f32),
        pltpu.VMEM((NH, 2, 256, 256), f32),
        pltpu.VMEM((NH, 2, 3, 64, 256), f32),
        pltpu.VMEM((NH, 2, 64, 256), f32),
        pltpu.VMEM((NH, 64, 256), f32),
        pltpu.VMEM((8, 128), i32),
        pltpu.VMEM((2, 8, 128), i32),
        pltpu.VMEM((8, 128), i32),
        pltpu.VMEM((3, 8, 128), i32),
        pltpu.VMEM((8, 128), i32),
    ]
    scratch += [pltpu.VMEM((4 * NW, 8, 128), f32) for _ in range(NH)]
    scratch += [pltpu.VMEM((4 * cz, 8, 128), f32) for _ in range(NH)]
    scratch += [pltpu.VMEM((4, cy, 8, 128), f32) for _ in range(NH)]
    scratch += [
        dma((4,)), dma((16,)), dma((6,)),
        dma((4,)), dma((4,)), dma((4,)), dma((4,)),
        dma((NH, 4)), dma((NH, 4)),
        dma((NH, 4)), dma((NH, 4)),
        dma((NH, 2, 2)), dma((NH, 2, 2)),
        dma((NH, 2)), dma((NH, 2)),
        dma((NH, 2)), dma((NH, 2)),
        dma((NH, 2, 4)), dma((NH, 2, 4)),
        dma((NH,)), dma((NH,)),
        dma((5,)), dma((5,)),
    ]
    return pl.pallas_call(
        functools.partial(kernel, cz, cy),
        out_shape=(jax.ShapeDtypeStruct((64, 1024), f32), jax.ShapeDtypeStruct((1, 1), i32)),
        in_specs=[any_] * 6,
        out_specs=(vmem, smem),
        scratch_shapes=scratch,
        compiler_params=pltpu.CompilerParams(
            collective_id=collective_id, has_side_effects=True, vmem_limit_bytes=56 * 2**20
        ),
    )(left, lp, win, rp, sub, sq)


def shards(left_blocks, left_pattern, right_window, right_pattern, subset_cols, square_cols):
    args = (
        left_blocks.reshape(1024 * NR, BS),
        left_pattern.reshape(8, NR),
        right_window.reshape(128, 2048),
        right_pattern.reshape(1, 16),
        subset_cols,
        square_cols,
    )
    fast, flag = run(18, 50, 0, *args)
    return lax.cond(
        flag[0, 0] > 0,
        lambda value, *rest: run(32, 128, 1, *rest)[0],
        lambda value, *rest: value,
        fast, *args,
    )


def solution(mesh):
    return jax.shard_map(
        shards,
        mesh=mesh,
        in_specs=(
            P("row", ("col", "depth"), None),
            P("row", ("col", "depth"), None),
            P(("col", "depth"), "row", None),
            P(("col", "depth"), "row", None),
            P(),
            P(("row", "col", "depth"), None),
        ),
        out_specs=P(("row", "col", "depth"), None),
        check_vma=False,
    )
```

```python
import functools

import jax
import jax.numpy as jnp
from jax import lax
from jax.experimental import pallas as pl
from jax.experimental.pallas import tpu as pltpu
from jax.sharding import PartitionSpec as P

MESH = pl.DeviceIdType.MESH
BS = 128
NH = 4
NW = 8
NR = 16


def dot_nt(a, b):
    return lax.dot_general(a, b, (((1,), (1,)), ((), ())), preferred_element_type=jnp.float32)


def kernel(cz, cy, left_h, lp_h, win_h, rp_h, sub_h, sq_h, out_v, flag_s, *scratch):
    (lp_s, rp_s, sub_s, sq_v, left_v, win_v, ahi, alo, spread, py_v, pz_v, one_v, one_s, idx_v, idx_s, bhi, blo,
     prod, cr, xr, vz, zx, fl_a, fl_b, fl_c, fl_x, fl_z,
     rec0, rec1, rec2, rec3, zr0, zr1, zr2, zr3, yr0, yr1, yr2, yr3,
     ssem, wsem, lsem, py_ss, py_rs, pz_ss, pz_rs, a_ss, a_rs, z_ss, z_rs, y_ss, y_rs, f_ss, f_rs,
     c_ss, c_rs, x_ss, x_rs, v_ss, v_rs, fl_ss, fl_rs) = scratch
    rec = (rec0, rec1, rec2, rec3)
    zr = (zr0, zr1, zr2, zr3)
    yr = (yr0, yr1, yr2, yr3)
    half = cy // 2

    r = lax.axis_index("row")
    x = lax.axis_index("col")
    d = lax.axis_index("depth")
    y = lax.rem(r, 4)
    z = r // 4
    core = lax.rem(d, 2)
    zh = d // 2

    def row_at(dz, dy):
        return lax.rem(z + dz, 4) * 4 + lax.rem(y + dy, 4)

    core_peer = {"depth": d + 1 - 2 * core}
    zh_peer = {"depth": lax.rem(d + 2, 4)}

    def x_peer(dx):
        return {"col": lax.rem(x + dx, 4)}

    def remote(src, dst, ss, rs, device):
        return pltpu.make_async_remote_copy(
            src_ref=src, dst_ref=dst, send_sem=ss, recv_sem=rs, device_id=device, device_id_type=MESH
        )

    barrier = pltpu.get_barrier_semaphore()
    for k in range(1, 4):
        pl.semaphore_signal(barrier, inc=1, device_id={"row": row_at(0, k)}, device_id_type=MESH)
        pl.semaphore_signal(barrier, inc=1, device_id={"row": row_at(k, 0)}, device_id_type=MESH)
        pl.semaphore_signal(barrier, inc=1, device_id=x_peer(k), device_id_type=MESH)
    pl.semaphore_signal(barrier, inc=1, device_id=core_peer, device_id_type=MESH)
    pl.semaphore_signal(barrier, inc=1, device_id=zh_peer, device_id_type=MESH)

    small = []
    for k, (src, dst) in enumerate(((sub_h, sub_s), (rp_h, rp_s), (lp_h, lp_s), (sq_h, sq_v))):
        cp = pltpu.make_async_copy(src, dst, ssem.at[k])
        cp.start()
        small.append(cp)
    win_copies = []
    for w in range(16):
        cp = pltpu.make_async_copy(win_h.at[:, pl.ds(w * BS, BS)], win_v.at[w], wsem.at[w])
        cp.start()
        win_copies.append(cp)
    left_copies = []
    for part in range(4):
        cp = pltpu.make_async_copy(
            left_h.at[pl.ds(part * 4096, 4096)], left_v.at[pl.ds(part * 4096, 4096)], lsem.at[1 + part]
        )
        cp.start()
        left_copies.append(cp)
    for cp in small:
        cp.wait()

    lane = lax.broadcasted_iota(jnp.int32, (8, 128), 1)
    mine = jnp.zeros((8, 128), jnp.int32)
    for w in range(NW):
        mine = jnp.where(lane == y * NW + w, rp_s[0, sub_s[w]], mine)
    py_v[y] = mine
    for cp in win_copies:
        cp.wait()
    for w in range(NW):
        block = win_v[sub_s[w]].T
        for h in range(NH):
            for to in range(4):
                at = 32 * h + 8 * to
                spread[h, to, w] = block[at:at + 8, :]
    pl.semaphore_wait(barrier, 11)

    pt = []
    for dy in (1, 3, 2):
        cp = remote(py_v.at[y], py_v.at[y], py_ss.at[dy], py_rs.at[dy], {"row": row_at(0, dy)})
        cp.start()
        pt.append(cp)

    a2a = []
    for h in range(NH):
        row = []
        for dy in (2, 1, 3):
            to = lax.rem(y + dy, 4)
            cp = remote(spread.at[h, to], rec[h].at[pl.ds(y * NW, NW)], a_ss.at[h, dy], a_rs.at[h, dy], {"row": row_at(0, dy)})
            cp.start()
            row.append(cp)
        a2a.append(row)
        rec[h][pl.ds(y * NW, NW)] = spread[h, y]

    def prepare(first):
        for cp in left_copies[first // 4:first // 4 + 2]:
            cp.wait()

        def body(piece, _):
            at = lax.rem(piece, 2) * 512 + lax.rem(piece // 2, 2) * 256 + (piece // 4) * 64
            at = pl.multiple_of(at, 64)
            for q in range(NR):
                v = left_v[pl.ds(piece * 1024 + q, 64, stride=16), :]
                v = jnp.where(jnp.full((64, 128), lp_s[piece // 2, q], jnp.int32) != 0, v, 0.0)
                hi = v.astype(jnp.bfloat16)
                ahi[pl.ds(at, 64), q * BS:(q + 1) * BS] = hi
                alo[pl.ds(at, 64), q * BS:(q + 1) * BS] = (v - hi.astype(jnp.float32)).astype(jnp.bfloat16)
            return 0

        lax.fori_loop(first, first + 8, body, 0)

    def column(v):
        return jnp.broadcast_to(v[0:1, :], (128, 128)).T

    for cp in pt:
        cp.wait_recv()
    pool = (py_v[0] + py_v[1]) + (py_v[2] + py_v[3])
    pz_v[z] = pool
    for dz in (1, 3, 2):
        cp = remote(pz_v.at[z], pz_v.at[z], pz_ss.at[dz], pz_rs.at[dz], {"row": row_at(dz, 0)})
        cp.start()
        pt.append(cp)
    upto = pool
    for s in (1, 2, 4, 8, 16):
        upto = upto + jnp.where(lane >= s, pltpu.roll(upto, s, 1), 0)
    blk = lax.broadcasted_iota(jnp.int32, (32, 128), 0)
    slot = lax.broadcasted_iota(jnp.int32, (32, 128), 1)
    place = jnp.where(pool != 0, upto - pool, 255)
    first = jnp.where(column(place)[0:32, :] == slot, blk, 0)
    one_v[...] = jnp.broadcast_to(jnp.sum(first, axis=0, keepdims=True), (8, 128))
    to_one = pltpu.make_async_copy(one_v, one_s, lsem.at[0])
    to_one.start()
    to_one.wait()

    zg = []
    for h in range(NH):
        for cp in a2a[h]:
            cp.wait_recv()

        def pack(j, _, h=h):
            at = one_s[0, j]
            zr[h][z * cz + j] = rec[h][at]
            return 0

        if cz <= 20:
            for j in range(cz):
                pack(j, 0)
        else:
            lax.fori_loop(0, cz, pack, 0)
        row = {}
        part = zr[h].at[pl.ds(z * cz, cz)]
        for dz in (2, 1, 3):
            row[dz] = remote(part, part, z_ss.at[h, dz], z_rs.at[h, dz], {"row": row_at(dz, 0)})
        row[2].start()

        @pl.when(z != 3)
        def _(cp=row[1]):
            cp.start()

        @pl.when(z != 0)
        def _(cp=row[3]):
            cp.start()

        zg.append(row)

    for cp in pt[3:]:
        cp.wait_recv()
    pat = jnp.where(lane < 32, pz_v[0], 0)
    for k in range(1, 4):
        pat = jnp.where(lane // 32 == k, pltpu.roll(pz_v[k], 32 * k, 1), pat)
    in_pool = lax.rem(lane, 32)
    c32 = pat
    for s in (1, 2, 4, 8, 16):
        c32 = c32 + jnp.where(in_pool >= s, pltpu.roll(c32, s, 1), 0)
    call = pat
    for s in (1, 2, 4, 8, 16, 32, 64):
        call = call + jnp.where(lane >= s, pltpu.roll(call, s, 1), 0)
    rank = call - pat
    zsrc = (lane // 32) * cz + jnp.minimum(c32 - pat, cz - 1)
    slot = lax.broadcasted_iota(jnp.int32, (128, 128), 1)
    second = jnp.where(column(jnp.where(pat != 0, rank, 255)) == slot, column(zsrc), 0)
    idx_v[0:2, :] = pat[0:2, :]
    idx_v[1:2, :] = jnp.sum(second, axis=0, keepdims=True)
    idx_v[2:3, :] = jnp.minimum(rank, cy - 1)[0:1, :]
    idx_v[3:4, :] = pat[0:1, :]
    idx_v[4:8, :] = pat[0:4, :]
    over = jnp.where((in_pool == 31) & (c32 > cz), 1, 0) + jnp.where((lane == 127) & (call > cy), 1, 0)
    for s in (1, 2, 4, 8, 16, 32, 64):
        over = over + pltpu.roll(over, s, 1)
    fl_a[...] = over
    to_s = pltpu.make_async_copy(idx_v, idx_s, lsem.at[5])
    to_s.start()
    to_s.wait()

    zf = []
    for h in range(NH):
        up = zr[h].at[pl.ds(0, cz)]
        down = zr[h].at[pl.ds(3 * cz, cz)]
        zf.append((
            remote(up, up, z_ss.at[h, 0], z_rs.at[h, 3], {"row": 12 + y}),
            remote(down, down, z_ss.at[h, 0], z_rs.at[h, 1], {"row": y}),
        ))

    def z_forward(h):
        zg[h][2].wait_recv()

        @pl.when(z == 2)
        def _():
            zf[h][0].start()

        @pl.when(z == 1)
        def _():
            zf[h][1].start()

    sides = ((0, 1), (1, 3))

    def yg(h, side, k):
        part = yr[h].at[y, pl.ds(k * half, half)]
        return remote(part, part, y_ss.at[h, side, k], y_rs.at[h, side, k], {"row": row_at(0, sides[side][1])})

    def fg(h, side):
        part = yr[h].at[lax.rem(y + (3 if side == 0 else 1), 4), pl.ds(side * half, half)]
        return remote(part, part, f_ss.at[h, side], f_rs.at[h, side], {"row": row_at(0, sides[side][1])})

    def y_send(h):
        zg[h][1].wait_recv()
        zg[h][3].wait_recv()

        def pack(j, _):
            at = idx_s[1, j]
            yr[h][y, j] = zr[h][at]
            return 0

        if cy <= 64:
            def ten(i, _):
                for k in range(10):
                    pack(i * 10 + k, 0)
                return 0

            lax.fori_loop(0, cy // 10, ten, 0)
        else:
            lax.fori_loop(0, cy, pack, 0)
        for side in (0, 1):
            for k in ((0, 1) if side == 0 else (1, 0)):
                yg(h, side, k).start()

    def y_forward(h):
        for side in (0, 1):
            yg(h, side, side).wait_recv()
            fg(h, side).start()

    def y_wait(h):
        for side in (0, 1):
            yg(h, side, 1 - side).wait_recv()
            fg(h, side).wait_recv()

    def expand(h):
        def body(w, _):
            at = pl.multiple_of(w * 32, 32)
            for q in range(NR):
                place = idx_s[2, q * NW + w]
                keep = jnp.full((32, 128), idx_s[3, q * NW + w], jnp.int32) != 0
                v = jnp.concatenate([yr[h][k, place] for k in range(4)], axis=0)
                v = jnp.where(keep, v, 0.0)
                hi = v.astype(jnp.bfloat16)
                bhi[pl.ds(at, 32), q * BS:(q + 1) * BS] = hi
                blo[pl.ds(at, 32), q * BS:(q + 1) * BS] = (v - hi.astype(jnp.float32)).astype(jnp.bfloat16)
            return 0

        lax.fori_loop(0, NW, body, 0)

    def product(s):
        swap_core = 1 - lax.rem(s, 2)
        swap_zh = 1 - lax.rem(s // 2, 2)
        core_to = core + swap_core * (1 - 2 * core)
        zh_to = zh + swap_zh * (1 - 2 * zh)
        at = pl.multiple_of(core_to * 512 + zh_to * 256, 256)
        a_hi, a_lo = ahi[pl.ds(at, 256), :], alo[pl.ds(at, 256), :]
        b_hi, b_lo = bhi[...], blo[...]
        return dot_nt(a_hi, b_hi) + dot_nt(a_hi, b_lo) + dot_nt(a_lo, b_hi)

    def cg(h, p):
        return remote(prod.at[4 * h + 2 * p], cr.at[h, p], c_ss.at[h, p], c_rs.at[h, p], core_peer)

    def xg(h, p, dx):
        part = prod.at[4 * h + 2 * p + 1, pl.ds(pl.multiple_of(lax.rem(x + dx, 4) * 64, 64), 64)]
        return remote(part, xr.at[h, p, dx - 1], x_ss.at[h, p, dx], x_rs.at[h, p, dx], x_peer(dx))

    def vg(h):
        return remote(vz.at[h, 0], zx.at[h], v_ss.at[h], v_rs.at[h], zh_peer)

    def flg(k):
        if k == 0:
            return remote(fl_a, fl_c, fl_ss.at[0], fl_rs.at[0], core_peer)
        if k == 4:
            return remote(fl_b.at[1], fl_z, fl_ss.at[4], fl_rs.at[4], zh_peer)
        return remote(fl_b.at[0], fl_x.at[k - 1], fl_ss.at[k], fl_rs.at[k], x_peer(k))

    def to_core(h, p):
        cg(h, p).start()
        if (h, p) == (0, 0):
            flg(0).start()

    def over_x(h, p):
        cg(h, p).wait_recv()
        prod[4 * h + 2 * p + 1] = prod[4 * h + 2 * p + 1] + cr[h, p]
        for dx in (2, 1, 3):
            xg(h, p, dx).start()
        if (h, p) == (0, 0):
            flg(0).wait_recv()
            fl_b[0] = fl_a[...] + fl_c[...]
            for dx in (1, 3, 2):
                flg(dx).start()

    def sum_x(h, p):
        total = prod[4 * h + 2 * p + 1, pl.ds(pl.multiple_of(x * 64, 64), 64), :]
        for dx in (1, 3, 2):
            xg(h, p, dx).wait_recv()
            total = total + xr[h, p, dx - 1]
        vz[h, p] = total

    def over_zh(h):
        sum_x(h, 0)
        vg(h).start()
        if h == 0:
            for dx in (1, 3, 2):
                flg(dx).wait_recv()
            fl_b[1] = (fl_b[0] + fl_x[0]) + (fl_x[1] + fl_x[2])
            flg(4).start()

    lane64 = lax.broadcasted_iota(jnp.int32, (64, 128), 1)

    def finish(h):
        vg(h).wait_recv()
        total = vz[h, 1] + zx[h]
        for w in range(NW):
            tile = total[:, (w // 4) * 128:(w // 4 + 1) * 128]
            shift = (32 * h - 32 * (w % 4)) % 128
            if shift:
                tile = pltpu.roll(tile, shift, 1)
            cols = slice(w * BS, (w + 1) * BS)
            value = 3.0 * sq_v[:, cols] - 2.0 * tile
            if h:
                value = jnp.where(lane64 // 32 == h, value, out_v[:, cols])
            out_v[:, cols] = value
        if h == 0:
            flg(4).wait_recv()
            one_v[...] = fl_b[1] + fl_z[...]
            to_flag = pltpu.make_async_copy(one_v, one_s, lsem.at[0])
            to_flag.start()
            to_flag.wait()
            flag_s[0, 0] = one_s[0, 0]

    prepare(0)
    z_forward(0)
    y_send(0)
    prepare(8)
    z_forward(1)
    y_forward(0)
    y_send(1)

    def step(s, _):
        for h in range(NH):
            @pl.when(s == 4 * h)
            def _(h=h):
                y_wait(h)
                expand(h)

        prod[s] = product(s)

        for h in range(NH):
            @pl.when(s == 4 * h)
            def _(h=h):
                to_core(h, 0)
                if h + 1 < NH:
                    y_forward(h + 1)
                if h + 2 < NH:
                    z_forward(h + 2)
                    y_send(h + 2)

            @pl.when(s == 4 * h + 1)
            def _(h=h):
                over_x(h, 0)

            @pl.when(s == 4 * h + 2)
            def _(h=h):
                to_core(h, 1)
                if h >= 1:
                    over_zh(h - 1)

            @pl.when(s == 4 * h + 3)
            def _(h=h):
                if h + 1 < NH:
                    if h >= 1:
                        sum_x(h - 1, 1)
                    over_x(h, 1)
                    if h >= 2:
                        finish(h - 2)

        return 0

    lax.fori_loop(0, 4 * NH, step, 0)
    over_x(NH - 1, 1)
    over_zh(NH - 1)
    sum_x(NH - 2, 1)
    finish(NH - 3)
    finish(NH - 2)
    sum_x(NH - 1, 1)
    finish(NH - 1)

    for cp in pt:
        cp.wait_send()
    for row in a2a:
        for cp in row:
            cp.wait_send()
    for row in zg:
        row[2].wait_send()

    @pl.when(z != 3)
    def _():
        for row in zg:
            row[1].wait_send()

    @pl.when(z != 0)
    def _():
        for row in zg:
            row[3].wait_send()

    @pl.when(z == 2)
    def _():
        for row in zf:
            row[0].wait_send()

    @pl.when(z == 1)
    def _():
        for row in zf:
            row[1].wait_send()

    for h in range(NH):
        for side in (0, 1):
            fg(h, side).wait_send()
            for k in (0, 1):
                yg(h, side, k).wait_send()
        for p in (0, 1):
            cg(h, p).wait_send()
            for dx in (1, 2, 3):
                xg(h, p, dx).wait_send()
        vg(h).wait_send()
    for k in range(5):
        flg(k).wait_send()


def run(cz, cy, collective_id, left, lp, win, rp, sub, sq):
    any_ = pl.BlockSpec(memory_space=pl.ANY)
    vmem = pl.BlockSpec(memory_space=pltpu.VMEM)
    smem = pl.BlockSpec(memory_space=pltpu.SMEM)
    f32, bf16, i32 = jnp.float32, jnp.bfloat16, jnp.int32
    dma = pltpu.SemaphoreType.DMA
    scratch = [
        pltpu.SMEM((8, NR), i32),
        pltpu.SMEM((1, 16), i32),
        pltpu.SMEM((8,), i32),
        pltpu.VMEM((64, 1024), f32),
        pltpu.VMEM((16384, 128), f32),
        pltpu.VMEM((16, 128, 128), f32),
        pltpu.VMEM((1024, 2048), bf16),
        pltpu.VMEM((1024, 2048), bf16),
        pltpu.VMEM((NH, 4, NW, 8, 128), f32),
        pltpu.VMEM((4, 8, 128), i32),
        pltpu.VMEM((4, 8, 128), i32),
        pltpu.VMEM((8, 128), i32),
        pltpu.SMEM((8, 128), i32),
        pltpu.VMEM((8, 128), i32),
        pltpu.SMEM((8, 128), i32),
        pltpu.VMEM((256, 2048), bf16),
        pltpu.VMEM((256, 2048), bf16),
        pltpu.VMEM((4 * NH, 256, 256), f32),
        pltpu.VMEM((NH, 2, 256, 256), f32),
        pltpu.VMEM((NH, 2, 3, 64, 256), f32),
        pltpu.VMEM((NH, 2, 64, 256), f32),
        pltpu.VMEM((NH, 64, 256), f32),
        pltpu.VMEM((8, 128), i32),
        pltpu.VMEM((2, 8, 128), i32),
        pltpu.VMEM((8, 128), i32),
        pltpu.VMEM((3, 8, 128), i32),
        pltpu.VMEM((8, 128), i32),
    ]
    scratch += [pltpu.VMEM((4 * NW, 8, 128), f32) for _ in range(NH)]
    scratch += [pltpu.VMEM((4 * cz, 8, 128), f32) for _ in range(NH)]
    scratch += [pltpu.VMEM((4, cy, 8, 128), f32) for _ in range(NH)]
    scratch += [
        dma((4,)), dma((16,)), dma((6,)),
        dma((4,)), dma((4,)), dma((4,)), dma((4,)),
        dma((NH, 4)), dma((NH, 4)),
        dma((NH, 4)), dma((NH, 4)),
        dma((NH, 2, 2)), dma((NH, 2, 2)),
        dma((NH, 2)), dma((NH, 2)),
        dma((NH, 2)), dma((NH, 2)),
        dma((NH, 2, 4)), dma((NH, 2, 4)),
        dma((NH,)), dma((NH,)),
        dma((5,)), dma((5,)),
    ]
    return pl.pallas_call(
        functools.partial(kernel, cz, cy),
        out_shape=(jax.ShapeDtypeStruct((64, 1024), f32), jax.ShapeDtypeStruct((1, 1), i32)),
        in_specs=[any_] * 6,
        out_specs=(vmem, smem),
        scratch_shapes=scratch,
        compiler_params=pltpu.CompilerParams(
            collective_id=collective_id, has_side_effects=True, vmem_limit_bytes=56 * 2**20
        ),
    )(left, lp, win, rp, sub, sq)


def shards(left_blocks, left_pattern, right_window, right_pattern, subset_cols, square_cols):
    args = (
        left_blocks.reshape(1024 * NR, BS),
        left_pattern.reshape(8, NR),
        right_window.reshape(128, 2048),
        right_pattern.reshape(1, 16),
        subset_cols,
        square_cols,
    )
    fast, flag = run(18, 50, 0, *args)
    return lax.cond(
        flag[0, 0] > 0,
        lambda value, *rest: run(32, 128, 1, *rest)[0],
        lambda value, *rest: value,
        fast, *args,
    )


def solution(mesh):
    return jax.shard_map(
        shards,
        mesh=mesh,
        in_specs=(
            P("row", ("col", "depth"), None),
            P("row", ("col", "depth"), None),
            P(("col", "depth"), "row", None),
            P(("col", "depth"), "row", None),
            P(),
            P(("row", "col", "depth"), None),
        ),
        out_specs=P(("row", "col", "depth"), None),
        check_vma=False,
    )
```
